128 devices in a mesh: seq: 16 (over x, y), head: 8 (over z, core).
Axes of the slice: x: 4, y: 4, z: 4, core: 2. Of those that a mesh axis runs over, the one named last changes fastest.
Arguments:
- query_proj: bfloat16 [49152, 5120], P('seq', 'head'), may hold values from -10 to 10
- key_proj: bfloat16 [49152, 5120], P('seq', 'head'), may hold values from -10 to 10
- value_proj: bfloat16 [49152, 5120], P('seq', 'head'), may hold values from -6 to 6
- query_gain: float32 [5120], P('head'), may hold values from 0.5 to 1.5
- key_gain: float32 [5120], P('head'), may hold values from 0.5 to 1.5
- head_class: int32 [40], P('head'), may hold values from 0 to 1, as said below
- spatial_mask: int32 [40, 12, 12], P('head'), may hold values 0 or 1
- temporal_mask: int32 [40, 8, 8], P('head'), may hold values 0 or 1
- location_order: int32 [1536], replicated, may hold values from 0 to 1535, each once
Outputs:
- attended: bfloat16 [49152, 5120], P('seq', 'head')
The draws below stay inside these ranges and needn't reach their ends.
Inputs may be any that keep to these rules, and one draw needn't show every extreme that they name: `head_class`: in every aligned group of 5 consecutive heads exactly 4 are temporal (1), the others spatial (0).
All inputs are finite; a program needn't handle non-finite values. No bound on the sum of `spatial_mask` or of `temporal_mask` on one device may be relied on, other than what follows from the above.
Results may differ from the reference program's by a relative error of at most 0.001.
The reference program's roundings to bfloat16 on the way count: a program that leaves them out, or rounds other values in their place, can miss the bound.
Values may be sent and summed in bfloat16 or wider, within the bound.
No kernel may reach another device: no remote copies, remote signals or barrier semaphores. Data moves between devices by JAX's collectives and lax.ppermute only.
A program may use at most 128 MiB of HBM per device.

```python
import jax
import jax.numpy as jnp
from jax import lax

HEADS = 40
HEAD_DIM = 128
LOCATIONS = 1536
BLOCK = 128
WINDOW_SPAN = 32
GROUP = 5
TEMPORAL = 4
FRAMES = 32
TOKENS = 49152
SPATIAL_BLOCKS = 12
WINDOW_BLOCKS = 8


def head_levels(ratio):
    position = jnp.arange(HEADS, dtype=jnp.float32) / (HEADS - 1)
    return 0.6 * ratio ** position


def draw_query_proj(key, part):
    key = jax.random.fold_in(key, 11)
    first_key = jax.random.fold_in(key, 0)
    entries = jnp.clip(jax.random.normal(first_key, (TOKENS, HEADS, HEAD_DIM), jnp.float32), -4.0, 4.0) * head_levels(3.0)[None, :, None]
    return entries.reshape(TOKENS, HEADS * HEAD_DIM).astype(jnp.bfloat16)


def draw_key_proj(key, part):
    key = jax.random.fold_in(key, 23)
    first_key = jax.random.fold_in(key, 0)
    entries = jnp.clip(jax.random.normal(first_key, (TOKENS, HEADS, HEAD_DIM), jnp.float32), -4.0, 4.0) * head_levels(3.0)[None, :, None]
    return entries.reshape(TOKENS, HEADS * HEAD_DIM).astype(jnp.bfloat16)


def draw_head_class(key, part):
    key = jax.random.fold_in(key, 37)
    group_keys = jax.random.split(key, HEADS // GROUP)

    def one_group(group_key):
        shuffled = jax.random.permutation(group_key, GROUP)
        return (shuffled < TEMPORAL).astype(jnp.int32)
    return jax.vmap(one_group)(group_keys).reshape(HEADS)


def plant(array, own_key, least, largest):
    index_at = [jax.random.randint(jax.random.fold_in(own_key, axis), (), 0, length) for axis, length in enumerate(array.shape)]
    longest = array.shape.index(max(array.shape))
    neighbour = index_at[:longest] + [(index_at[longest] + 1) % array.shape[longest]] + index_at[longest + 1:]
    return array.at[tuple(index_at)].set(least).at[tuple(neighbour)].set(largest)


def block_levels(key, shape, cuts, low, largest):
    def one(dim, shards_of):
        steps = jax.random.uniform(jax.random.fold_in(jax.random.fold_in(key, 6), dim), (shards_of,), jnp.float32, low / len(cuts), largest / len(cuts))
        return jnp.repeat(jnp.exp(steps), shape[dim] // shards_of).reshape((-1,) + (1,) * (len(shape) - dim - 1))

    factor_of = one(*cuts[0])
    for cut in cuts[1:]:
        factor_of = factor_of * one(*cut)
    return factor_of


def gaussian(own_key, dims, width, most, cuts=(), kind=jnp.bfloat16):
    values = width * jax.random.normal(own_key, dims, jnp.float32)
    if cuts:
        values = values * block_levels(own_key, dims, cuts, -0.22, 0.18)
    return jnp.clip(values, -most, most).astype(kind)


def setup_inputs(seed: int = 0) -> dict:
    seeds = jax.random.split(jax.random.key(seed), 10)
    return {
        "query_proj": draw_query_proj(jax.random.fold_in(seeds[9], 71), 0),
        "key_proj": draw_key_proj(jax.random.fold_in(seeds[9], 71), 0),
        "value_proj": gaussian(seeds[2], (TOKENS, HEADS * HEAD_DIM), 1.0, 6.0, ((0, 16), (1, 8))),
        "query_gain": jnp.clip(1.0 + 0.1 * jax.random.normal(seeds[3], (HEADS * HEAD_DIM,), jnp.float32), 0.5, 1.5),
        "key_gain": jnp.clip(1.0 + 0.1 * jax.random.normal(seeds[4], (HEADS * HEAD_DIM,), jnp.float32), 0.5, 1.5),
        "head_class": draw_head_class(jax.random.fold_in(seeds[9], 71), 0),
        "spatial_mask": plant((jax.random.randint(seeds[6], (HEADS, SPATIAL_BLOCKS, SPATIAL_BLOCKS), 0, 2) < 1).astype(jnp.int32), jax.random.fold_in(seeds[6], 1), 0, 1),
        "temporal_mask": plant((jax.random.randint(seeds[7], (HEADS, WINDOW_BLOCKS, WINDOW_BLOCKS), 0, 2) < 1).astype(jnp.int32), jax.random.fold_in(seeds[7], 1), 0, 1),
        "location_order": jax.random.permutation(seeds[8], LOCATIONS).astype(jnp.int32),
    }


EPSILON = 1e-06

def normalized(projected, gain):
    values = projected.astype(jnp.float32)
    mean_square = lax.optimization_barrier(jnp.mean(values * values, axis=1, keepdims=True))
    rounded = (values * lax.rsqrt(mean_square + EPSILON) * gain.astype(jnp.float32)).astype(jnp.bfloat16)
    return lax.optimization_barrier(rounded)

def expand_mask(block_mask):
    blocks = block_mask.shape[-1]
    diagonal = jnp.arange(blocks, dtype=jnp.int32)[:, None] == jnp.arange(blocks, dtype=jnp.int32)[None, :]
    kept_mask = (block_mask != 0) | diagonal
    widened = jnp.broadcast_to(kept_mask[:, None, :, None], (blocks, BLOCK, blocks, BLOCK))
    return widened.reshape(blocks * BLOCK, blocks * BLOCK)

def attend(queries, key_rows, values, allowed):
    scaling = HEAD_DIM ** (-0.5)
    scores = jnp.einsum('gqd,gkd->gqk', queries.astype(jnp.float32), key_rows.astype(jnp.float32)) * scaling
    scores = jnp.where(allowed, scores, -jnp.inf)
    row_top = lax.optimization_barrier(jnp.max(scores, axis=-1, keepdims=True))
    weights = jnp.where(allowed, jnp.exp(scores - row_top), 0.0)
    totals = lax.optimization_barrier(jnp.sum(weights, axis=-1, keepdims=True))
    rounded_weights = lax.optimization_barrier(weights.astype(jnp.bfloat16)).astype(jnp.float32)
    mixture = jnp.einsum('gqk,gkd->gqd', rounded_weights, values.astype(jnp.float32))
    return (mixture / totals).astype(jnp.bfloat16)

def reference(query_proj, key_proj, value_proj, query_gain, key_gain, head_class, spatial_mask, temporal_mask, location_order):
    grid_shape = (FRAMES, LOCATIONS, HEADS, HEAD_DIM)
    query_heads = jnp.moveaxis(normalized(query_proj, query_gain).reshape(grid_shape), 2, 0)
    key_heads = jnp.moveaxis(normalized(key_proj, key_gain).reshape(grid_shape), 2, 0)
    value_heads = jnp.moveaxis(value_proj.reshape(grid_shape), 2, 0)
    inverse = jnp.zeros((LOCATIONS,), jnp.int32).at[location_order].set(jnp.arange(LOCATIONS, dtype=jnp.int32))

    def arrange(tensor):
        relaid = jnp.take(tensor, location_order, axis=1)
        return jnp.transpose(relaid, (1, 0, 2)).reshape(LOCATIONS // WINDOW_SPAN, WINDOW_SPAN * FRAMES, HEAD_DIM)

    def spatial_side(member):
        queries, key_rows, values, spatial_blocks, temporal_blocks = member
        return attend(queries, key_rows, values, expand_mask(spatial_blocks))

    def temporal_side(member):
        queries, key_rows, values, spatial_blocks, temporal_blocks = member
        mixture = attend(arrange(queries), arrange(key_rows), arrange(values), expand_mask(temporal_blocks))
        ordered = jnp.transpose(mixture.reshape(LOCATIONS, FRAMES, HEAD_DIM), (1, 0, 2))
        return jnp.take(ordered, inverse, axis=1)

    def one_head(member):
        head_kind = member[0]
        return lax.cond(head_kind == 1, temporal_side, spatial_side, member[1:])
    result = lax.map(one_head, (head_class, query_heads, key_heads, value_heads, spatial_mask, temporal_mask))
    return jnp.moveaxis(result, 0, 2).reshape(TOKENS, HEADS * HEAD_DIM)
```

```python
import functools

import jax
import jax.numpy as jnp
from jax import lax
from jax.experimental import pallas as pl
from jax.experimental.pallas import tpu as pltpu
from jax.sharding import PartitionSpec as P

HEADS = 40
HEAD_DIM = 128
LOCATIONS = 1536
BLOCK = 128
WINDOW_SPAN = 32
GROUP = 5
TEMPORAL = 4
FEATURES = HEADS * HEAD_DIM
EPSILON = 1e-06
MASKED = -1e30
EXP2_SCALE = 1.4426950408889634 * HEAD_DIM ** (-0.5)
LANE_BLOCKS = LOCATIONS // 128
VMEM_LIMIT = 40 * 2**20

F32 = jnp.float32
BF16 = jnp.bfloat16


def params(vmem=VMEM_LIMIT):
    return pltpu.CompilerParams(vmem_limit_bytes=vmem)


def cost(flops, nbytes, exps=0):
    return pl.CostEstimate(flops=int(flops), bytes_accessed=int(nbytes), transcendentals=int(exps))


def spatial_head(class_ref):
    found = jnp.int32(0)
    for i in range(1, GROUP):
        found = found + i * (1 - class_ref[i])
    return found


def temporal_head(class_ref, j):
    return j + (j >= spatial_head(class_ref)).astype(jnp.int32)


def column(row):
    return jnp.broadcast_to(row, (128, 128)).T


def sums_kernel(q_ref, k_ref, out_ref):
    for a, ref in enumerate((q_ref, k_ref)):
        for i in range(q_ref.shape[0] // 128):
            part = jnp.zeros((128, 128), F32)
            for j in range(GROUP):
                x = ref[128 * i : 128 * i + 128, 128 * j : 128 * j + 128].astype(F32)
                part = part + x * x
            out_ref[a, 0, i, :] = jnp.sum(part.T, axis=0)


def square_sums(query_proj, key_proj):
    tokens, features = query_proj.shape
    frames = tokens // LOCATIONS
    in_spec = pl.BlockSpec((LOCATIONS, features), lambda f: (f, 0))
    return pl.pallas_call(
        sums_kernel,
        grid=(frames,),
        in_specs=[in_spec, in_spec],
        out_specs=pl.BlockSpec((2, 1, LANE_BLOCKS, 128), lambda f: (0, f, 0, 0)),
        out_shape=jax.ShapeDtypeStruct((2, frames, LANE_BLOCKS, 128), F32),
        compiler_params=params(),
        cost_estimate=cost(4 * tokens * features, 4 * tokens * features),
        name="square_sums",
    )(query_proj, key_proj)


def build_picked(order_ref, picked_ref):
    lanes = lax.broadcasted_iota(jnp.int32, (128, 128), 1).astype(F32)
    for i in range(LANE_BLOCKS):
        wanted = column(order_ref[i : i + 1, :].astype(F32))
        for j in range(LANE_BLOCKS):
            hit = wanted == lanes + float(128 * j)
            picked_ref[128 * i : 128 * i + 128, 128 * j : 128 * j + 128] = jnp.where(
                hit, 1.0, 0.0
            ).astype(BF16)


def pick_rows(picked_ref, heads_ref, store):
    rows = 384
    for c in range(LOCATIONS // rows):
        y = jnp.dot(
            picked_ref[rows * c : rows * c + rows, :],
            heads_ref[...],
            preferred_element_type=F32,
        ).astype(BF16)
        store(c, rows, y)


def pack_value_kernel(class_ref, order_ref, x_ref, out_ref, picked_ref, heads_ref):
    @pl.when(pl.program_id(0) == 0)
    def _():
        build_picked(order_ref, picked_ref)

    for j in range(TEMPORAL):
        h = temporal_head(class_ref, j)
        heads_ref[:, 128 * j : 128 * j + 128] = x_ref[
            :, pl.ds(pl.multiple_of(h * 128, 128), 128)
        ]

    def store(c, rows, y):
        slots = rows // 96
        for j in range(TEMPORAL):
            out_ref[slots * c : slots * c + slots, j, 0] = y[
                :, 128 * j : 128 * j + 128
            ].reshape(slots, 96, 128)

    pick_rows(picked_ref, heads_ref, store)


def pack_values(value_proj, head_class, order):
    tokens, features = value_proj.shape
    frames = tokens // LOCATIONS
    return pl.pallas_call(
        pack_value_kernel,
        grid_spec=pltpu.PrefetchScalarGridSpec(
            num_scalar_prefetch=1,
            grid=(frames,),
            in_specs=[
                pl.BlockSpec((LANE_BLOCKS, 128), lambda f, c: (0, 0)),
                pl.BlockSpec((LOCATIONS, features), lambda f, c: (f, 0)),
            ],
            out_specs=pl.BlockSpec((16, TEMPORAL, 1, 96, 128), lambda f, c: (0, 0, f, 0, 0)),
            scratch_shapes=[
                pltpu.VMEM((LOCATIONS, LOCATIONS), BF16),
                pltpu.VMEM((LOCATIONS, TEMPORAL * 128), BF16),
            ],
        ),
        out_shape=jax.ShapeDtypeStruct((16, TEMPORAL, frames, 96, 128), BF16),
        compiler_params=params(),
        cost_estimate=cost(2 * tokens * LOCATIONS * 512, 4 * tokens * features),
        name="pack_values",
    )(head_class, order, value_proj)


def factor_of(sums):
    return lax.rsqrt(sums * (1.0 / FEATURES) + EPSILON)


def pack_norm_kernel(
    split, class_ref, order_ref, sums_ref, gain_ref, q_ref, k_ref, *rest
):
    out_refs, (picked_ref, heads_ref) = rest[:-2], rest[-2:]

    @pl.when((pl.program_id(0) == 0) & (pl.program_id(1) == 0))
    def _():
        build_picked(order_ref, picked_ref)

    def load(x_ref):
        factor = factor_of(sums_ref[0, 0])
        for i in range(LANE_BLOCKS):
            scale = column(factor[i : i + 1, :])
            for j in range(TEMPORAL):
                h = pl.multiple_of(temporal_head(class_ref, j) * 128, 128)
                x = x_ref[128 * i : 128 * i + 128, pl.ds(h, 128)].astype(F32)
                gain = gain_ref[0, :, pl.ds(h, 128)]
                heads_ref[128 * i : 128 * i + 128, 128 * j : 128 * j + 128] = (
                    x * scale * gain
                ).astype(BF16)

    @pl.when(pl.program_id(0) == 0)
    def _():
        load(q_ref)

    @pl.when(pl.program_id(0) == 1)
    def _():
        load(k_ref)

    def store(c, rows, y):
        slots = rows // 96
        j = 0
        for out_ref, count in zip(out_refs, split):
            for i in range(count):
                out_ref[slots * c : slots * c + slots, i, 0, 0] = y[
                    :, 128 * j : 128 * j + 128
                ].reshape(slots, 96, 128)
                j += 1

    pick_rows(picked_ref, heads_ref, store)


def pack_norms(query_proj, key_proj, sums, gains, head_class, order, split):
    tokens, features = query_proj.shape
    frames = tokens // LOCATIONS
    return pl.pallas_call(
        functools.partial(pack_norm_kernel, split),
        grid_spec=pltpu.PrefetchScalarGridSpec(
            num_scalar_prefetch=1,
            grid=(2, frames),
            in_specs=[
                pl.BlockSpec((LANE_BLOCKS, 128), lambda a, f, c: (0, 0)),
                pl.BlockSpec((1, 1, LANE_BLOCKS, 128), lambda a, f, c: (a, f, 0, 0)),
                pl.BlockSpec((1, 1, features), lambda a, f, c: (a, 0, 0)),
                pl.BlockSpec((LOCATIONS, features), lambda a, f, c: (f * (1 - a) + a * (frames - 1), 0)),
                pl.BlockSpec((LOCATIONS, features), lambda a, f, c: (f * a, 0)),
            ],
            out_specs=[
                pl.BlockSpec((16, n, 1, 1, 96, 128), lambda a, f, c: (0, 0, a, f, 0, 0))
                for n in split
            ],
            scratch_shapes=[
                pltpu.VMEM((LOCATIONS, LOCATIONS), BF16),
                pltpu.VMEM((LOCATIONS, TEMPORAL * 128), BF16),
            ],
        ),
        out_shape=[jax.ShapeDtypeStruct((16, n, 2, frames, 96, 128), BF16) for n in split],
        compiler_params=params(),
        cost_estimate=cost(4 * tokens * LOCATIONS * 512, 8 * tokens * features),
        name="pack_norms",
    )(head_class, order, sums, gains, query_proj, key_proj)


def softmax_rows(queries, key_rows, values, bias):
    s = lax.dot_general(
        queries, key_rows, (((1,), (1,)), ((), ())), preferred_element_type=F32
    )
    rows, keys = s.shape
    s = (s.reshape(-1, *bias.shape) + bias).reshape(rows, keys)
    top = jnp.max(s, axis=1, keepdims=True)
    w = jnp.exp2((s - top) * EXP2_SCALE)
    total = jnp.sum(w, axis=1, keepdims=True)
    mixture = jnp.dot(w.astype(BF16), values, preferred_element_type=F32)
    return (mixture / total).astype(BF16)


def window_kernel(class_ref, bias_ref, q_ref, k_ref, v_ref, *rest):
    out_ref = rest[-1]
    tokens = 16 * 2 * WINDOW_SPAN
    q = q_ref[...].reshape(tokens, 128)
    k = k_ref[...].reshape(tokens, 128)
    v = v_ref[...].reshape(tokens, 128)
    bias = bias_ref[0]
    rows = 256
    for c in range(tokens // rows):
        o = softmax_rows(q[rows * c : rows * c + rows], k, v, bias)
        slots = rows // (2 * WINDOW_SPAN)
        out_ref[slots * c : slots * c + slots, 0] = o.reshape(slots, 2, WINDOW_SPAN, 128)


def window_attention(moved, values, bias, head_class, first, before):
    count = moved.shape[1]
    windows = 96 // WINDOW_SPAN
    block = (16, 1, 2, WINDOW_SPAN, 128)
    qk_block = (16, 1, 1, 2, WINDOW_SPAN, 128)
    in_specs = [
        pl.BlockSpec(
            (1, WINDOW_SPAN, 1024), lambda h, w, c: (temporal_head(c, h + first), 0, 0)
        ),
        pl.BlockSpec(qk_block, lambda h, w, c: (0, h, 0, 0, w, 0)),
        pl.BlockSpec(qk_block, lambda h, w, c: (0, h, 1, 0, w, 0)),
        pl.BlockSpec(block, lambda h, w, c: (0, h + first, 0, w, 0)),
    ]
    operands = [head_class, bias, moved, moved, values]
    aliases = {}
    if before is not None:
        in_specs.append(pl.BlockSpec(memory_space=pl.ANY))
        aliases = {len(operands): 0}
        operands.append(before)
    return pl.pallas_call(
        window_kernel,
        grid_spec=pltpu.PrefetchScalarGridSpec(
            num_scalar_prefetch=1,
            grid=(count, windows),
            in_specs=in_specs,
            out_specs=pl.BlockSpec(block, lambda h, w, c: (0, h + first, 0, w, 0)),
        ),
        out_shape=jax.ShapeDtypeStruct((16, TEMPORAL, 2, 96, 128), BF16),
        input_output_aliases=aliases,
        compiler_params=params(),
        cost_estimate=cost(
            8 * count * windows * 1024 * 1024 * 128, 8 * count * windows * 1024 * 128, count * windows * 1024 * 1024
        ),
        name="window_attention",
    )(*operands)


def frame_kernel(class_ref, bias_ref, sums_ref, gain_ref, q_ref, k_ref, v_ref, out_ref, qn_ref, kn_ref):
    for a, (x_ref, n_ref) in enumerate(((q_ref, qn_ref), (k_ref, kn_ref))):
        factor = factor_of(sums_ref[a, 0])
        for i in range(LANE_BLOCKS):
            x = x_ref[128 * i : 128 * i + 128, :].astype(F32)
            n_ref[128 * i : 128 * i + 128, :] = (
                x * column(factor[i : i + 1, :]) * gain_ref[a]
            ).astype(BF16)

    def body(i, carry):
        rows = pl.ds(pl.multiple_of(i * 128, 128), 128)
        out_ref[rows, :] = softmax_rows(
            qn_ref[rows, :], kn_ref[...], v_ref[...], bias_ref[0, pl.ds(i, 1), :]
        )
        return carry

    lax.fori_loop(0, LANE_BLOCKS, body, 0)


def frame_attention(query_proj, key_proj, value_proj, sums, gains, bias, head_class):
    tokens = query_proj.shape[0]
    frames = tokens // LOCATIONS
    column_spec = pl.BlockSpec((LOCATIONS, 128), lambda f, c: (f, spatial_head(c)))
    return pl.pallas_call(
        frame_kernel,
        grid_spec=pltpu.PrefetchScalarGridSpec(
            num_scalar_prefetch=1,
            grid=(frames,),
            in_specs=[
                pl.BlockSpec((1, LANE_BLOCKS, LOCATIONS), lambda f, c: (spatial_head(c), 0, 0)),
                pl.BlockSpec((2, 1, LANE_BLOCKS, 128), lambda f, c: (0, f, 0, 0)),
                pl.BlockSpec((2, 1, 128), lambda f, c: (0, 0, spatial_head(c))),
                column_spec,
                column_spec,
                column_spec,
            ],
            out_specs=pl.BlockSpec((LOCATIONS, 128), lambda f, c: (f, 0)),
            scratch_shapes=[
                pltpu.VMEM((LOCATIONS, 128), BF16),
                pltpu.VMEM((LOCATIONS, 128), BF16),
            ],
        ),
        out_shape=jax.ShapeDtypeStruct((tokens, 128), BF16),
        compiler_params=params(),
        cost_estimate=cost(
            4 * tokens * LOCATIONS * 256, 8 * tokens * 128, tokens * LOCATIONS
        ),
        name="frame_attention",
    )(head_class, bias, sums, gains, query_proj, key_proj, value_proj)


def unpack_kernel(class_ref, order_ref, spatial_ref, moved_ref, out_ref, heads_ref):
    rows = out_ref.shape[0]
    first = pl.program_id(1) * rows
    for j in range(TEMPORAL):
        heads_ref[:, 128 * j : 128 * j + 128] = moved_ref[:, j, 0].reshape(LOCATIONS, 128)
    places = lax.broadcasted_iota(jnp.int32, (rows, 128), 0) + first
    parts = []
    for i in range(LANE_BLOCKS):
        hit = order_ref[i : i + 1, :] == places
        parts.append(jnp.where(hit, 1.0, 0.0).astype(BF16))
    y = jnp.dot(
        jnp.concatenate(parts, axis=1), heads_ref[...], preferred_element_type=F32
    ).astype(BF16)
    for j in range(TEMPORAL):
        h = pl.multiple_of(temporal_head(class_ref, j) * 128, 128)
        out_ref[:, pl.ds(h, 128)] = y[:, 128 * j : 128 * j + 128]
    h = pl.multiple_of(spatial_head(class_ref) * 128, 128)
    out_ref[:, pl.ds(h, 128)] = spatial_ref[...]


def unpack(returned, spatial_out, head_class, order):
    frames = returned.shape[2]
    tokens = frames * LOCATIONS
    rows = 768
    steps = LOCATIONS // rows
    return pl.pallas_call(
        unpack_kernel,
        grid_spec=pltpu.PrefetchScalarGridSpec(
            num_scalar_prefetch=1,
            grid=(frames, steps),
            in_specs=[
                pl.BlockSpec((LANE_BLOCKS, 128), lambda f, i, c: (0, 0)),
                pl.BlockSpec((rows, 128), lambda f, i, c: (f * steps + i, 0)),
                pl.BlockSpec((16, TEMPORAL, 1, 96, 128), lambda f, i, c: (0, 0, f, 0, 0)),
            ],
            out_specs=pl.BlockSpec((rows, GROUP * 128), lambda f, i, c: (f * steps + i, 0)),
            scratch_shapes=[pltpu.VMEM((LOCATIONS, TEMPORAL * 128), BF16)],
        ),
        out_shape=jax.ShapeDtypeStruct((tokens, GROUP * 128), BF16),
        compiler_params=params(),
        cost_estimate=cost(2 * tokens * LOCATIONS * 512, 4 * tokens * 640),
        name="unpack",
    )(head_class, order, spatial_out, returned)


def spread_mask(mask, repeat):
    blocks = mask.shape[-1]
    same = jnp.arange(blocks)[:, None] == jnp.arange(blocks)[None, :]
    bias = jnp.where((mask != 0) | same, 0.0, MASKED).astype(F32)
    return jnp.repeat(bias, repeat, axis=2)


def exchange(tensor):
    return lax.all_to_all(tensor, "seq", split_axis=0, concat_axis=0, tiled=True)


SPLIT = (3, 1)


def shards(
    query_proj,
    key_proj,
    value_proj,
    query_gain,
    key_gain,
    head_class,
    spatial_mask,
    temporal_mask,
    location_order,
):
    order = location_order.reshape(LANE_BLOCKS, 128)
    gains = jnp.stack([query_gain, key_gain])[:, None, :]
    window_bias = jnp.tile(
        jnp.repeat(spread_mask(temporal_mask, 4), 4, axis=1), (1, 1, 32)
    )
    frame_bias = spread_mask(spatial_mask, 128)

    packed_values = pack_values(value_proj, head_class, order)
    sums = square_sums(query_proj, key_proj)
    values = exchange(packed_values)
    sums = lax.psum(sums, "head")
    packed = pack_norms(query_proj, key_proj, sums, gains, head_class, order, SPLIT)
    values, *packed = lax.optimization_barrier((values, *packed))

    moved = exchange(packed[0])
    spatial_out = frame_attention(
        query_proj, key_proj, value_proj, sums, gains, frame_bias, head_class
    )
    moved, spatial_out, later = lax.optimization_barrier((moved, spatial_out, packed[1]))

    moved_later = exchange(later)
    mixed = window_attention(moved, values, window_bias, head_class, 0, None)
    mixed, moved_later = lax.optimization_barrier((mixed, moved_later))

    mixed = window_attention(moved_later, values, window_bias, head_class, SPLIT[0], mixed)
    returned = exchange(mixed)
    return unpack(returned, spatial_out, head_class, order)


def solution(mesh):
    return jax.shard_map(
        shards,
        mesh=mesh,
        in_specs=(
            P("seq", "head"),
            P("seq", "head"),
            P("seq", "head"),
            P("head"),
            P("head"),
            P("head"),
            P("head", None, None),
            P("head", None, None),
            P(),
        ),
        out_specs=P("seq", "head"),
        check_vma=False,
    )
```

```python
import functools

import jax
import jax.numpy as jnp
from jax import lax
from jax.experimental import pallas as pl
from jax.experimental.pallas import tpu as pltpu
from jax.sharding import PartitionSpec as P

HEADS = 40
HEAD_DIM = 128
LOCATIONS = 1536
BLOCK = 128
WINDOW_SPAN = 32
GROUP = 5
TEMPORAL = 4
FEATURES = HEADS * HEAD_DIM
EPSILON = 1e-06
MASKED = -(2.0**100)
EXP2_SCALE = 1.4426950408889634 * HEAD_DIM ** (-0.5)
LANE_BLOCKS = LOCATIONS // 128
PAIR = 2
VMEM_LIMIT = 60 * 2**20

F32 = jnp.float32
BF16 = jnp.bfloat16


def params(vmem=VMEM_LIMIT):
    return pltpu.CompilerParams(vmem_limit_bytes=vmem)


def cost(flops, nbytes, exps=0):
    return pl.CostEstimate(flops=int(flops), bytes_accessed=int(nbytes), transcendentals=int(exps))


def spatial_head(class_ref):
    found = jnp.int32(0)
    for i in range(1, GROUP):
        found = found + i * (1 - class_ref[i])
    return found


def temporal_head(class_ref, j):
    return j + (j >= spatial_head(class_ref)).astype(jnp.int32)


def column(row):
    return jnp.broadcast_to(row, (128, 128)).T


def sums_kernel(q_ref, k_ref, out_ref):
    for a, ref in enumerate((q_ref, k_ref)):
        for i in range(q_ref.shape[0] // 128):
            part = jnp.zeros((128, 128), F32)
            for j in range(GROUP):
                x = ref[128 * i : 128 * i + 128, 128 * j : 128 * j + 128].astype(F32)
                part = part + x * x
            out_ref[a, 0, 0, i, :] = jnp.sum(part.T, axis=0)


def square_sums(query_proj, key_proj):
    tokens, features = query_proj.shape
    frames = tokens // LOCATIONS
    parts = 3
    in_spec = pl.BlockSpec((LOCATIONS // parts, features), lambda f, i: (f * parts + i, 0))
    return pl.pallas_call(
        sums_kernel,
        grid=(frames, parts),
        in_specs=[in_spec, in_spec],
        out_specs=pl.BlockSpec(
            (2, 1, 1, LANE_BLOCKS // parts, 128), lambda f, i: (0, f, i, 0, 0)
        ),
        out_shape=jax.ShapeDtypeStruct((2, frames, parts, LANE_BLOCKS // parts, 128), F32),
        compiler_params=params(),
        cost_estimate=cost(4 * tokens * features, 4 * tokens * features),
        name="square_sums",
    )(query_proj, key_proj)


def build_picked(order_ref, picked_ref):
    lanes = lax.broadcasted_iota(jnp.int32, (128, 128), 1).astype(F32)
    for i in range(LANE_BLOCKS):
        wanted = column(order_ref[i : i + 1, :].astype(F32))
        for j in range(LANE_BLOCKS):
            hit = wanted == lanes + float(128 * j)
            picked_ref[128 * i : 128 * i + 128, 128 * j : 128 * j + 128] = jnp.where(
                hit, 1.0, 0.0
            ).astype(BF16)


def pick_rows(picked_ref, heads_ref, store):
    rows = 384
    for c in range(LOCATIONS // rows):
        y = jnp.dot(
            picked_ref[rows * c : rows * c + rows, :],
            heads_ref[...],
            preferred_element_type=F32,
        ).astype(BF16)
        store(c, rows, y)


def pack_value_kernel(class_ref, order_ref, x_ref, out_ref, picked_ref, heads_ref):
    @pl.when(pl.program_id(0) == 0)
    def _():
        build_picked(order_ref, picked_ref)

    for j in range(TEMPORAL):
        h = temporal_head(class_ref, j)
        heads_ref[:, 128 * j : 128 * j + 128] = x_ref[
            :, pl.ds(pl.multiple_of(h * 128, 128), 128)
        ]

    def store(c, rows, y):
        slots = rows // 96
        for j in range(TEMPORAL):
            out_ref[slots * c : slots * c + slots, j, 0] = y[
                :, 128 * j : 128 * j + 128
            ].reshape(slots, 96, 128)

    pick_rows(picked_ref, heads_ref, store)


def pack_values(value_proj, head_class, order):
    tokens, features = value_proj.shape
    frames = tokens // LOCATIONS
    return pl.pallas_call(
        pack_value_kernel,
        grid_spec=pltpu.PrefetchScalarGridSpec(
            num_scalar_prefetch=1,
            grid=(frames,),
            in_specs=[
                pl.BlockSpec((LANE_BLOCKS, 128), lambda f, c: (0, 0)),
                pl.BlockSpec((LOCATIONS, features), lambda f, c: (f, 0)),
            ],
            out_specs=pl.BlockSpec((16, TEMPORAL, 1, 96, 128), lambda f, c: (0, 0, f, 0, 0)),
            scratch_shapes=[
                pltpu.VMEM((LOCATIONS, LOCATIONS), BF16),
                pltpu.VMEM((LOCATIONS, TEMPORAL * 128), BF16),
            ],
        ),
        out_shape=jax.ShapeDtypeStruct((16, TEMPORAL, frames, 96, 128), BF16),
        compiler_params=params(),
        cost_estimate=cost(2 * tokens * LOCATIONS * 512, 4 * tokens * features),
        name="pack_values",
    )(head_class, order, value_proj)


def factor_of(sums):
    return lax.rsqrt(sums * (1.0 / FEATURES) + EPSILON)


def pack_norm_kernel(
    class_ref, turn_ref, order_ref, sums_ref, gain0_ref, gain1_ref, q0_ref, q1_ref, k0_ref, k1_ref, *rest
):
    before_ref, (out_ref, picked_ref, heads_ref) = rest[:-3], rest[-3:]
    mine = turn_ref[0] != 0
    array = pl.program_id(0)

    @pl.when(mine & (array == 0) & (pl.program_id(1) == 0))
    def _():
        build_picked(order_ref, picked_ref)

    def load(refs):
        factor = factor_of(sums_ref[0, 0])
        for i in range(LANE_BLOCKS):
            scale = column(factor[i : i + 1, :])
            for j, (x_ref, gain_ref) in enumerate(zip(refs, (gain0_ref, gain1_ref))):
                x = x_ref[128 * i : 128 * i + 128, :].astype(F32)
                heads_ref[128 * i : 128 * i + 128, 128 * j : 128 * j + 128] = (
                    x * scale * gain_ref[0]
                ).astype(BF16)

    @pl.when(mine & (array == 0))
    def _():
        load((q0_ref, q1_ref))

    @pl.when(mine & (array == 1))
    def _():
        load((k0_ref, k1_ref))

    @pl.when(mine)
    def _():
        def store(c, rows, y):
            slots = rows // 96
            for j in range(PAIR):
                out_ref[slots * c : slots * c + slots, j, 0, 0] = y[
                    :, 128 * j : 128 * j + 128
                ].reshape(slots, 96, 128)

        pick_rows(picked_ref, heads_ref, store)

    if before_ref:

        @pl.when(jnp.logical_not(mine))
        def _():
            out_ref[...] = before_ref[0][...]


def pack_norms(query_proj, key_proj, sums, gains, head_class, order, first, turn, before=None):
    tokens, features = query_proj.shape
    frames = tokens // LOCATIONS

    def head_spec(array, j):
        def index(a, f, c, t):
            frame = f * (1 - a) + a * (frames - 1) if array == 0 else f * a
            return (frame * t[0], temporal_head(c, first + j))

        return pl.BlockSpec((LOCATIONS, 128), index)

    def gain_spec(j):
        return pl.BlockSpec((1, 1, 128), lambda a, f, c, t: (a, 0, temporal_head(c, first + j)))

    out_spec = pl.BlockSpec(
        (16, PAIR, 1, 1, 96, 128), lambda a, f, c, t: (0, 0, a * t[0], f * t[0], 0, 0)
    )
    in_specs = [
        pl.BlockSpec((LANE_BLOCKS, 128), lambda a, f, c, t: (0, 0)),
        pl.BlockSpec((1, 1, LANE_BLOCKS, 128), lambda a, f, c, t: (a, f, 0, 0)),
        gain_spec(0),
        gain_spec(1),
        head_spec(0, 0),
        head_spec(0, 1),
        head_spec(1, 0),
        head_spec(1, 1),
    ]
    operands = [
        head_class, turn, order, sums, gains, gains, query_proj, query_proj, key_proj, key_proj
    ]
    aliases = {}
    if before is not None:
        in_specs.append(
            pl.BlockSpec((16, PAIR, 1, 1, 96, 128), lambda a, f, c, t: (0, 0, 0, 0, 0, 0))
        )
        aliases = {len(operands): 0}
        operands.append(before)
    return pl.pallas_call(
        pack_norm_kernel,
        grid_spec=pltpu.PrefetchScalarGridSpec(
            num_scalar_prefetch=2,
            grid=(2, frames),
            in_specs=in_specs,
            out_specs=out_spec,
            scratch_shapes=[
                pltpu.VMEM((LOCATIONS, LOCATIONS), BF16),
                pltpu.VMEM((LOCATIONS, PAIR * 128), BF16),
            ],
        ),
        out_shape=jax.ShapeDtypeStruct((16, PAIR, 2, frames, 96, 128), BF16),
        input_output_aliases=aliases,
        compiler_params=params(),
        cost_estimate=cost(4 * tokens * LOCATIONS * 256, 8 * tokens * 256),
        name="pack_norms",
    )(*operands)


def softmax_rows(queries, key_rows, values, bias=None):
    s = lax.dot_general(
        queries, key_rows, (((1,), (1,)), ((), ())), preferred_element_type=F32
    )
    if bias is not None:
        s = s + bias
    top = jnp.max(s, axis=1, keepdims=True)
    w = jnp.exp2((s - top) * EXP2_SCALE)
    total = jnp.sum(w, axis=1, keepdims=True)
    mixture = jnp.dot(w.astype(BF16), values, preferred_element_type=F32)
    return (mixture / total).astype(BF16)


def window_kernel(class_ref, bias_ref, q_ref, k_ref, v_ref, out_ref, wide_q_ref, wide_k_ref):
    tokens = 16 * 2 * WINDOW_SPAN

    @pl.when((pl.program_id(0) == 0) & (pl.program_id(1) == 0))
    def _():
        place = lax.broadcasted_iota(jnp.int32, (tokens, 128), 0) % WINDOW_SPAN
        lane = lax.broadcasted_iota(jnp.int32, (tokens, 128), 1)
        wide_q_ref[:, 128:] = jnp.where(place // 4 == lane, 1.0, 0.0).astype(BF16)

    @pl.when(pl.program_id(1) == 0)
    def _():
        repeated = jnp.broadcast_to(bias_ref[...], (32, WINDOW_SPAN, 128))
        wide_k_ref[:, 128:] = repeated.reshape(tokens, 128).astype(BF16)

    wide_q_ref[:, :128] = q_ref[...].reshape(tokens, 128)
    wide_k_ref[:, :128] = k_ref[...].reshape(tokens, 128)
    v = v_ref[...].reshape(tokens, 128)
    rows = 256
    for c in range(tokens // rows):
        o = softmax_rows(wide_q_ref[rows * c : rows * c + rows, :], wide_k_ref[...], v)
        slots = rows // (2 * WINDOW_SPAN)
        out_ref[slots * c : slots * c + slots, 0] = o.reshape(slots, 2, WINDOW_SPAN, 128)


def window_attention(moved, values, bias, head_class, first):
    count = moved.shape[1]
    windows = 96 // WINDOW_SPAN
    block = (16, 1, 2, WINDOW_SPAN, 128)
    qk_block = (16, 1, 1, 2, WINDOW_SPAN, 128)
    return pl.pallas_call(
        window_kernel,
        grid_spec=pltpu.PrefetchScalarGridSpec(
            num_scalar_prefetch=1,
            grid=(count, windows),
            in_specs=[
                pl.BlockSpec(
                    (1, WINDOW_SPAN, 128), lambda h, w, c: (temporal_head(c, h + first), 0, 0)
                ),
                pl.BlockSpec(qk_block, lambda h, w, c: (0, h, 0, 0, w, 0)),
                pl.BlockSpec(qk_block, lambda h, w, c: (0, h, 1, 0, w, 0)),
                pl.BlockSpec(block, lambda h, w, c: (0, h + first, 0, w, 0)),
            ],
            out_specs=pl.BlockSpec(block, lambda h, w, c: (0, h, 0, w, 0)),
            scratch_shapes=[
                pltpu.VMEM((16 * 2 * WINDOW_SPAN, 256), BF16),
                pltpu.VMEM((16 * 2 * WINDOW_SPAN, 256), BF16),
            ],
        ),
        out_shape=jax.ShapeDtypeStruct((16, count, 2, 96, 128), BF16),
        compiler_params=params(),
        cost_estimate=cost(
            8 * count * windows * 1024 * 1024 * 128, 8 * count * windows * 1024 * 128, count * windows * 1024 * 1024
        ),
        name="window_attention",
    )(head_class, bias, moved, moved, values)


def frame_kernel(class_ref, turn_ref, bias_ref, sums_ref, gain_ref, q_ref, k_ref, v_ref, *rest):
    before_ref, (out_ref, qn_ref, kn_ref) = rest[:-3], rest[-3:]

    @pl.when(turn_ref[0] != 0)
    def _():
        for a, (x_ref, n_ref) in enumerate(((q_ref, qn_ref), (k_ref, kn_ref))):
            factor = factor_of(sums_ref[a, 0])
            for i in range(LANE_BLOCKS):
                x = x_ref[128 * i : 128 * i + 128, :].astype(F32)
                n_ref[128 * i : 128 * i + 128, :] = (
                    x * column(factor[i : i + 1, :]) * gain_ref[a]
                ).astype(BF16)

        def body(i, carry):
            rows = pl.ds(pl.multiple_of(i * 128, 128), 128)
            out_ref[rows, :] = softmax_rows(
                qn_ref[rows, :], kn_ref[...], v_ref[...], bias_ref[0, pl.ds(i, 1), :]
            )
            return carry

        lax.fori_loop(0, LANE_BLOCKS, body, 0)

    if before_ref:

        @pl.when(turn_ref[0] == 0)
        def _():
            out_ref[...] = before_ref[0][...]


def frame_attention(query_proj, key_proj, value_proj, sums, gains, bias, head_class, turn, before=None):
    tokens = query_proj.shape[0]
    frames = tokens // LOCATIONS
    column_spec = pl.BlockSpec((LOCATIONS, 128), lambda f, c, t: (f * t[0], spatial_head(c)))
    out_spec = pl.BlockSpec((LOCATIONS, 128), lambda f, c, t: (f * t[0], 0))
    in_specs = [
        pl.BlockSpec((1, LANE_BLOCKS, LOCATIONS), lambda f, c, t: (spatial_head(c), 0, 0)),
        pl.BlockSpec((2, 1, LANE_BLOCKS, 128), lambda f, c, t: (0, f, 0, 0)),
        pl.BlockSpec((2, 1, 128), lambda f, c, t: (0, 0, spatial_head(c))),
        column_spec,
        column_spec,
        column_spec,
    ]
    operands = [head_class, turn, bias, sums, gains, query_proj, key_proj, value_proj]
    aliases = {}
    if before is not None:
        in_specs.append(pl.BlockSpec((LOCATIONS, 128), lambda f, c, t: (0, 0)))
        aliases = {len(operands): 0}
        operands.append(before)
    return pl.pallas_call(
        frame_kernel,
        grid_spec=pltpu.PrefetchScalarGridSpec(
            num_scalar_prefetch=2,
            grid=(frames,),
            in_specs=in_specs,
            out_specs=out_spec,
            scratch_shapes=[
                pltpu.VMEM((LOCATIONS, 128), BF16),
                pltpu.VMEM((LOCATIONS, 128), BF16),
            ],
        ),
        out_shape=jax.ShapeDtypeStruct((tokens, 128), BF16),
        input_output_aliases=aliases,
        compiler_params=params(),
        cost_estimate=cost(
            4 * tokens * LOCATIONS * 256, 8 * tokens * 128, tokens * LOCATIONS
        ),
        name="frame_attention",
    )(*operands)


def place_rows(order_ref, moved_ref, heads_ref, first, rows):
    count = moved_ref.shape[1]
    for j in range(count):
        heads_ref[:, 128 * j : 128 * j + 128] = moved_ref[:, j, 0].reshape(LOCATIONS, 128)
    places = lax.broadcasted_iota(jnp.int32, (rows, 128), 0) + first
    parts = []
    for i in range(LANE_BLOCKS):
        hit = order_ref[i : i + 1, :] == places
        parts.append(jnp.where(hit, 1.0, 0.0).astype(BF16))
    return jnp.dot(
        jnp.concatenate(parts, axis=1), heads_ref[...], preferred_element_type=F32
    ).astype(BF16)


def unpack_kernel(order_ref, moved_ref, out_ref, heads_ref):
    rows = out_ref.shape[0]
    out_ref[...] = place_rows(order_ref, moved_ref, heads_ref, pl.program_id(1) * rows, rows)


def join_kernel(class_ref, order_ref, moved_ref, early_ref, spatial_ref, out_ref, heads_ref):
    rows = out_ref.shape[0]
    y = place_rows(order_ref, moved_ref, heads_ref, pl.program_id(1) * rows, rows)
    early = early_ref.shape[1] // 128
    for j in range(TEMPORAL):
        h = pl.multiple_of(temporal_head(class_ref, j) * 128, 128)
        if j < early:
            out_ref[:, pl.ds(h, 128)] = early_ref[:, 128 * j : 128 * j + 128]
        else:
            i = j - early
            out_ref[:, pl.ds(h, 128)] = y[:, 128 * i : 128 * i + 128]
    h = pl.multiple_of(spatial_head(class_ref) * 128, 128)
    out_ref[:, pl.ds(h, 128)] = spatial_ref[...]


UNPACK_ROWS = 768


def unpack(returned, order):
    count, frames = returned.shape[1:3]
    tokens = frames * LOCATIONS
    rows = UNPACK_ROWS
    steps = LOCATIONS // rows
    return pl.pallas_call(
        unpack_kernel,
        grid=(frames, steps),
        in_specs=[
            pl.BlockSpec((LANE_BLOCKS, 128), lambda f, i: (0, 0)),
            pl.BlockSpec((16, count, 1, 96, 128), lambda f, i: (0, 0, f, 0, 0)),
        ],
        out_specs=pl.BlockSpec((rows, count * 128), lambda f, i: (f * steps + i, 0)),
        scratch_shapes=[pltpu.VMEM((LOCATIONS, count * 128), BF16)],
        out_shape=jax.ShapeDtypeStruct((tokens, count * 128), BF16),
        compiler_params=params(),
        cost_estimate=cost(2 * tokens * LOCATIONS * 128 * count, 4 * tokens * 128 * count),
        name="unpack",
    )(order, returned)


def join(returned, early, spatial_out, head_class, order):
    count, frames = returned.shape[1:3]
    tokens = frames * LOCATIONS
    rows = UNPACK_ROWS
    steps = LOCATIONS // rows
    return pl.pallas_call(
        join_kernel,
        grid_spec=pltpu.PrefetchScalarGridSpec(
            num_scalar_prefetch=1,
            grid=(frames, steps),
            in_specs=[
                pl.BlockSpec((LANE_BLOCKS, 128), lambda f, i, c: (0, 0)),
                pl.BlockSpec((16, count, 1, 96, 128), lambda f, i, c: (0, 0, f, 0, 0)),
                pl.BlockSpec((rows, early.shape[1]), lambda f, i, c: (f * steps + i, 0)),
                pl.BlockSpec((rows, 128), lambda f, i, c: (f * steps + i, 0)),
            ],
            out_specs=pl.BlockSpec((rows, GROUP * 128), lambda f, i, c: (f * steps + i, 0)),
            scratch_shapes=[pltpu.VMEM((LOCATIONS, count * 128), BF16)],
        ),
        out_shape=jax.ShapeDtypeStruct((tokens, GROUP * 128), BF16),
        compiler_params=params(),
        cost_estimate=cost(2 * tokens * LOCATIONS * 128 * count, 4 * tokens * 640),
        name="join",
    )(head_class, order, returned, early, spatial_out)


def spread_mask(mask, repeat):
    blocks = mask.shape[-1]
    same = jnp.arange(blocks)[:, None] == jnp.arange(blocks)[None, :]
    bias = jnp.where((mask != 0) | same, 0.0, MASKED).astype(F32)
    return jnp.repeat(bias, repeat, axis=2)


def exchange(tensor):
    return lax.all_to_all(tensor, "seq", split_axis=0, concat_axis=0, tiled=True)


def sum_over_heads(sums):
    size = lax.axis_size("head")
    step = 1
    while step < size:
        pairs = [(i, i ^ step) for i in range(size)]
        sums = sums + lax.ppermute(sums, "head", pairs)
        step *= 2
    return sums


def shards(
    query_proj,
    key_proj,
    value_proj,
    query_gain,
    key_gain,
    head_class,
    spatial_mask,
    temporal_mask,
    location_order,
):
    order = location_order.reshape(LANE_BLOCKS, 128)
    gains = jnp.stack([query_gain, key_gain])[:, None, :]
    window_bias = jnp.pad(
        jnp.repeat(jnp.swapaxes(spread_mask(temporal_mask, 1), 1, 2), 4, axis=1),
        ((0, 0), (0, 0), (0, 120)),
    )
    frame_bias = spread_mask(spatial_mask, 128)
    late = (lax.axis_index("head") % 2).astype(jnp.int32).reshape(1)
    always = jnp.ones((1,), jnp.int32)

    def norms(first, turn, before=None):
        return pack_norms(
            query_proj, key_proj, sums, gains, head_class, order, first, turn, before
        )

    def within_frames(turn, before=None):
        return frame_attention(
            query_proj, key_proj, value_proj, sums, gains, frame_bias, head_class, turn, before
        )

    packed_values = pack_values(value_proj, head_class, order)
    values = exchange(packed_values)
    query_proj, key_proj, packed_values = lax.optimization_barrier(
        (query_proj, key_proj, packed_values)
    )
    sums = sum_over_heads(square_sums(query_proj, key_proj)).reshape(2, -1, LANE_BLOCKS, 128)
    first = norms(0, always)
    second = norms(PAIR, late)
    spatial_out = within_frames(late)
    values, first, second, spatial_out = lax.optimization_barrier(
        (values, first, second, spatial_out)
    )

    moved = exchange(first)
    second = norms(PAIR, 1 - late, second)
    spatial_out = within_frames(1 - late, spatial_out)
    moved, spatial_out, second = lax.optimization_barrier((moved, spatial_out, second))

    moved_later = exchange(second)
    mixed = window_attention(moved, values, window_bias, head_class, 0)
    mixed, moved_later = lax.optimization_barrier((mixed, moved_later))

    returned = exchange(mixed)
    mixed = window_attention(moved_later, values, window_bias, head_class, PAIR)
    returned, mixed = lax.optimization_barrier((returned, mixed))

    last = exchange(mixed)
    early = unpack(returned, order)
    last, early = lax.optimization_barrier((last, early))
    return join(last, early, spatial_out, head_class, order)


def solution(mesh):
    return jax.shard_map(
        shards,
        mesh=mesh,
        in_specs=(
            P("seq", "head"),
            P("seq", "head"),
            P("seq", "head"),
            P("head"),
            P("head"),
            P("head"),
            P("head", None, None),
            P("head", None, None),
            P(),
        ),
        out_specs=P("seq", "head"),
        check_vma=False,
    )
```

```python
import functools

import jax
import jax.numpy as jnp
from jax import lax
from jax.experimental import pallas as pl
from jax.experimental.pallas import tpu as pltpu
from jax.sharding import PartitionSpec as P

HEADS = 40
HEAD_DIM = 128
LOCATIONS = 1536
BLOCK = 128
WINDOW_SPAN = 32
GROUP = 5
TEMPORAL = 4
FEATURES = HEADS * HEAD_DIM
EPSILON = 1e-06
MASKED = -(2.0**100)
EXP2_SCALE = 1.4426950408889634 * HEAD_DIM ** (-0.5)
LANE_BLOCKS = LOCATIONS // 128
PAIR = 2
VMEM_LIMIT = 52 * 2**20

F32 = jnp.float32
BF16 = jnp.bfloat16


def params(vmem=VMEM_LIMIT):
    return pltpu.CompilerParams(vmem_limit_bytes=vmem)


def cost(flops, nbytes, exps=0):
    return pl.CostEstimate(flops=int(flops), bytes_accessed=int(nbytes), transcendentals=int(exps))


def spatial_head(class_ref):
    found = jnp.int32(0)
    for i in range(1, GROUP):
        found = found + i * (1 - class_ref[i])
    return found


def temporal_head(class_ref, j):
    return j + (j >= spatial_head(class_ref)).astype(jnp.int32)


def column(row):
    return jnp.broadcast_to(row, (128, 128)).T


def sums_kernel(q_ref, k_ref, out_ref):
    for a, ref in enumerate((q_ref, k_ref)):
        for i in range(q_ref.shape[0] // 128):
            part = jnp.zeros((128, 128), F32)
            for j in range(GROUP):
                x = ref[128 * i : 128 * i + 128, 128 * j : 128 * j + 128].astype(F32)
                part = part + x * x
            out_ref[a, 0, i, :] = jnp.sum(part.T, axis=0)


def square_sums(query_proj, key_proj):
    tokens, features = query_proj.shape
    frames = tokens // LOCATIONS
    in_spec = pl.BlockSpec((LOCATIONS, features), lambda f: (f, 0))
    return pl.pallas_call(
        sums_kernel,
        grid=(frames,),
        in_specs=[in_spec, in_spec],
        out_specs=pl.BlockSpec((2, 1, LANE_BLOCKS, 128), lambda f: (0, f, 0, 0)),
        out_shape=jax.ShapeDtypeStruct((2, frames, LANE_BLOCKS, 128), F32),
        compiler_params=params(),
        cost_estimate=cost(4 * tokens * features, 4 * tokens * features),
        name="square_sums",
    )(query_proj, key_proj)


def build_picked(order_ref, picked_ref):
    lanes = lax.broadcasted_iota(jnp.int32, (128, 128), 1).astype(F32)

    def body(i, carry):
        wanted = column(order_ref[pl.ds(i, 1), :].astype(F32))
        rows = pl.ds(pl.multiple_of(i * 128, 128), 128)
        for j in range(LANE_BLOCKS):
            hit = wanted == lanes + float(128 * j)
            picked_ref[rows, 128 * j : 128 * j + 128] = jnp.where(hit, 1.0, 0.0).astype(BF16)
        return carry

    lax.fori_loop(0, LANE_BLOCKS, body, 0)


def pick_rows(picked_ref, heads, store):
    rows = 384
    for c in range(LOCATIONS // rows):
        y = jnp.dot(
            picked_ref[rows * c : rows * c + rows, :], heads, preferred_element_type=F32
        ).astype(BF16)
        store(c, rows, y)


def factor_of(sums):
    return lax.rsqrt(sums * (1.0 / FEATURES) + EPSILON)


def norm_steps(first, class_ref, sums_ref, gain_ref, x_refs, out_ref, scratch):
    picked_ref, heads_ref, in_ref, packed_ref, in_sem, out_sem = scratch
    frames = sums_ref.shape[1]
    steps = 2 * frames

    def head(j):
        return pl.multiple_of(temporal_head(class_ref, first + j) * 128, 128)

    def fetch(x_ref, f, n, j):
        return pltpu.make_async_copy(
            x_ref.at[pl.ds(pl.multiple_of(LOCATIONS * f, LOCATIONS), LOCATIONS), pl.ds(head(j), 128)],
            in_ref.at[n * PAIR + j],
            in_sem.at[n * PAIR + j],
        )

    def send(n):
        return pltpu.make_async_copy(
            packed_ref.at[n], out_ref.at[:, :, n // frames, n % frames], out_sem.at[n]
        )

    def arrived(n):
        for j in range(PAIR):
            fetch(x_refs[0], n % frames, n, j).wait()

    def scale(n, i):
        factor = column(factor_of(sums_ref[n // frames, n % frames, i : i + 1, :]))
        rows = slice(128 * i, 128 * i + 128)
        for j in range(PAIR):
            x = in_ref[n * PAIR + j, rows, :].astype(F32)
            gain = gain_ref[n // frames, :, pl.ds(head(j), 128)]
            heads_ref[n % 2, rows, 128 * j : 128 * j + 128] = (x * factor * gain).astype(BF16)

    def products_of(n, also):
        def store(c, rows, y):
            slots = rows // 96
            for j in range(PAIR):
                packed_ref[n, slots * c : slots * c + slots, j] = y[
                    :, 128 * j : 128 * j + 128
                ].reshape(slots, 96, 128)
            if also:
                for i in range(rows * c // 128, rows * (c + 1) // 128):
                    scale(n + 1, i)

        pick_rows(picked_ref, heads_ref[n % 2], store)
        send(n).start()

    def body(n, carry):
        arrived(n + 1)
        products_of(n, True)
        return carry

    for n in range(steps):
        for j in range(PAIR):
            fetch(x_refs[n // frames], n % frames, n, j).start()
    arrived(0)
    for i in range(LANE_BLOCKS):
        scale(0, i)
    lax.fori_loop(0, steps - 1, body, 0)
    products_of(steps - 1, False)
    for n in range(steps):
        send(n).wait()


def pack_norm_kernel(
    first, class_ref, turn_ref, order_ref, sums_ref, gain_ref, q_ref, k_ref, *rest
):
    @pl.when(turn_ref[0] != 0)
    def _():
        build_picked(order_ref, rest[-6])
        norm_steps(first, class_ref, sums_ref, gain_ref, (q_ref, k_ref), rest[-7], rest[-6:])


def front_kernel(
    class_ref, odd_ref, order_ref, sums_ref, gain_ref, q_ref, k_ref, v_ref, *rest
):
    norm_ref, out_ref = rest[:2]
    scratch, (v_in_ref, v_packed_ref, v_in_sem, v_out_sem) = rest[2:8], rest[8:]
    picked_ref = scratch[0]
    frames = sums_ref.shape[1]
    rows = 384
    chunks = LOCATIONS // rows
    slots = rows // 96

    def fetch(f, j):
        h = pl.multiple_of(temporal_head(class_ref, j) * 128, 128)
        return pltpu.make_async_copy(
            v_ref.at[pl.ds(LOCATIONS * f, LOCATIONS), pl.ds(h, 128)],
            v_in_ref.at[f, :, pl.ds(128 * j, 128)],
            v_in_sem.at[f * TEMPORAL + j],
        )

    def send(f, c):
        return pltpu.make_async_copy(
            v_packed_ref.at[f, pl.ds(slots * c, slots)],
            out_ref.at[pl.ds(slots * c, slots), :, f],
            v_out_sem.at[f * chunks + c],
        )

    for f in range(frames):
        for j in range(TEMPORAL):
            fetch(f, j).start()

    build_picked(order_ref, picked_ref)

    @pl.when(odd_ref[0] != 0)
    def _():
        norm_steps(0, class_ref, sums_ref, gain_ref, (q_ref, k_ref), norm_ref, scratch)

    for f in range(frames):
        for j in range(TEMPORAL):
            fetch(f, j).wait()

        def store(c, rows, y):
            for j in range(TEMPORAL):
                v_packed_ref[f, slots * c : slots * c + slots, j] = y[
                    :, 128 * j : 128 * j + 128
                ].reshape(slots, 96, 128)
            send(f, c).start()

        pick_rows(picked_ref, v_in_ref[f], store)
    for f in range(frames):
        for c in range(chunks):
            send(f, c).wait()


def pack_specs(frames, features):
    anywhere = pl.BlockSpec(memory_space=pl.ANY)
    in_specs = [
        pl.BlockSpec((LANE_BLOCKS, 128), lambda i, c, t: (0, 0)),
        pl.BlockSpec((2, frames, LANE_BLOCKS, 128), lambda i, c, t: (0, 0, 0, 0)),
        pl.BlockSpec((2, 1, features), lambda i, c, t: (0, 0, 0)),
        anywhere,
        anywhere,
    ]
    scratch = [
        pltpu.VMEM((LOCATIONS, LOCATIONS), BF16),
        pltpu.VMEM((2, LOCATIONS, PAIR * 128), BF16),
        pltpu.VMEM((2 * frames * PAIR, LOCATIONS, 128), BF16),
        pltpu.VMEM((2 * frames, 16, PAIR, 96, 128), BF16),
        pltpu.SemaphoreType.DMA((2 * frames * PAIR,)),
        pltpu.SemaphoreType.DMA((2 * frames,)),
    ]
    norms = jax.ShapeDtypeStruct((16, PAIR, 2, frames, 96, 128), BF16)
    return in_specs, scratch, norms, anywhere


def pack_front(query_proj, key_proj, value_proj, sums, gains, head_class, order, odd):
    tokens, features = query_proj.shape
    frames = tokens // LOCATIONS
    in_specs, scratch, norms, anywhere = pack_specs(frames, features)
    chunks = LOCATIONS // 384
    return pl.pallas_call(
        front_kernel,
        grid_spec=pltpu.PrefetchScalarGridSpec(
            num_scalar_prefetch=2,
            grid=(1,),
            in_specs=[*in_specs, anywhere],
            out_specs=[anywhere, anywhere],
            scratch_shapes=[
                *scratch,
                pltpu.VMEM((frames, LOCATIONS, TEMPORAL * 128), BF16),
                pltpu.VMEM((frames, 16, TEMPORAL, 96, 128), BF16),
                pltpu.SemaphoreType.DMA((frames * TEMPORAL,)),
                pltpu.SemaphoreType.DMA((frames * chunks,)),
            ],
        ),
        out_shape=[norms, jax.ShapeDtypeStruct((16, TEMPORAL, frames, 96, 128), BF16)],
        compiler_params=params(),
        cost_estimate=cost(6 * tokens * LOCATIONS * 256, 12 * tokens * 256),
        name="pack_front",
    )(head_class, odd, order, sums, gains, query_proj, key_proj, value_proj)


def pack_norms(query_proj, key_proj, sums, gains, head_class, order, first, turn, before=None):
    tokens, features = query_proj.shape
    frames = tokens // LOCATIONS
    in_specs, scratch, norms, anywhere = pack_specs(frames, features)
    operands = [head_class, turn, order, sums, gains, query_proj, key_proj]
    aliases = {}
    if before is not None:
        in_specs.append(anywhere)
        aliases = {len(operands): 0}
        operands.append(before)
    return pl.pallas_call(
        functools.partial(pack_norm_kernel, first),
        grid_spec=pltpu.PrefetchScalarGridSpec(
            num_scalar_prefetch=2,
            grid=(1,),
            in_specs=in_specs,
            out_specs=anywhere,
            scratch_shapes=scratch,
        ),
        out_shape=norms,
        input_output_aliases=aliases,
        compiler_params=params(),
        cost_estimate=cost(4 * tokens * LOCATIONS * 256, 8 * tokens * 256),
        name="pack_norms",
    )(*operands)


def attend(count, scores, values, store):
    s = scores(0)
    for c in range(count):
        later = scores(c + 1) if c + 1 < count else None
        top = jnp.max(s, axis=1, keepdims=True)
        w = jnp.exp2((s - top) * EXP2_SCALE)
        total = jnp.sum(w, axis=1, keepdims=True)
        mixture = jnp.dot(w.astype(BF16), values(c), preferred_element_type=F32)
        store(c, (mixture / total).astype(BF16))
        s = later


def products(queries, key_rows):
    return lax.dot_general(
        queries, key_rows, (((1,), (1,)), ((), ())), preferred_element_type=F32
    )


def window_kernel(class_ref, bias_ref, q_ref, k_ref, v_ref, *rest):
    out_ref, wide_q_ref, wide_k_ref = rest[-3:]
    tokens = 16 * 2 * WINDOW_SPAN
    windows = 96 // WINDOW_SPAN

    @pl.when(pl.program_id(0) == 0)
    def _():
        place = lax.broadcasted_iota(jnp.int32, (tokens, 128), 0) % WINDOW_SPAN
        lane = lax.broadcasted_iota(jnp.int32, (tokens, 128), 1)
        own = jnp.where(place // 4 == lane, 1.0, 0.0).astype(BF16)
        for w in range(windows):
            wide_q_ref[w, :, 128:] = own

    repeated = jnp.broadcast_to(bias_ref[...], (32, WINDOW_SPAN, 128))
    repeated = repeated.reshape(tokens, 128).astype(BF16)
    for w in range(windows):
        rows = slice(WINDOW_SPAN * w, WINDOW_SPAN * w + WINDOW_SPAN)
        wide_q_ref[w, :, :128] = q_ref[:, 0, 0, :, rows, :].reshape(tokens, 128)
        wide_k_ref[w, :, :128] = k_ref[:, 0, 0, :, rows, :].reshape(tokens, 128)
        wide_k_ref[w, :, 128:] = repeated

    rows = 256
    parts = tokens // rows

    def scores(c):
        w, r = divmod(c, parts)
        return products(wide_q_ref[w, rows * r : rows * r + rows, :], wide_k_ref[w])

    def values(c):
        w = c // parts
        return v_ref[:, 0, :, WINDOW_SPAN * w : WINDOW_SPAN * w + WINDOW_SPAN, :].reshape(
            tokens, 128
        )

    def store(c, o):
        w, r = divmod(c, parts)
        slots = rows // (2 * WINDOW_SPAN)
        out_ref[
            slots * r : slots * r + slots, 0, :, WINDOW_SPAN * w : WINDOW_SPAN * w + WINDOW_SPAN, :
        ] = o.reshape(slots, 2, WINDOW_SPAN, 128)

    attend(windows * parts, scores, values, store)


def window_attention(moved, values, bias, head_class, first, before=None):
    count = moved.shape[1]
    windows = 96 // WINDOW_SPAN
    tokens = 16 * 2 * WINDOW_SPAN
    qk_block = (16, 1, 1, 2, 96, 128)
    in_specs = [
        pl.BlockSpec((1, WINDOW_SPAN, 128), lambda h, c: (temporal_head(c, h + first), 0, 0)),
        pl.BlockSpec(qk_block, lambda h, c: (0, h, 0, 0, 0, 0)),
        pl.BlockSpec(qk_block, lambda h, c: (0, h, 1, 0, 0, 0)),
        pl.BlockSpec((16, 1, 2, 96, 128), lambda h, c: (0, h + first, 0, 0, 0)),
    ]
    operands = [head_class, bias, moved, moved, values]
    aliases = {}
    if before is not None:
        in_specs.append(pl.BlockSpec(memory_space=pl.ANY))
        aliases = {len(operands): 0}
        operands.append(before)
    return pl.pallas_call(
        window_kernel,
        grid_spec=pltpu.PrefetchScalarGridSpec(
            num_scalar_prefetch=1,
            grid=(count,),
            in_specs=in_specs,
            out_specs=pl.BlockSpec((16, 1, 2, 96, 128), lambda h, c: (0, h + first, 0, 0, 0)),
            scratch_shapes=[
                pltpu.VMEM((windows, tokens, 256), BF16),
                pltpu.VMEM((windows, tokens, 256), BF16),
            ],
        ),
        out_shape=jax.ShapeDtypeStruct((16, TEMPORAL, 2, 96, 128), BF16),
        input_output_aliases=aliases,
        compiler_params=params(),
        cost_estimate=cost(
            8 * count * windows * tokens * tokens * 128,
            8 * count * windows * tokens * 128,
            count * windows * tokens * tokens,
        ),
        name="window_attention",
    )(*operands)


def frame_kernel(
    class_ref, bias_ref, sums_ref, qg_ref, kg_ref, q_ref, k_ref, v_ref, out_ref, wide_q_ref, wide_k_ref
):
    lane = lax.broadcasted_iota(jnp.int32, (128, 128), 1)
    streams = ((q_ref, qg_ref, wide_q_ref), (k_ref, kg_ref, wide_k_ref))
    for a, (x_ref, gain_ref, wide_ref) in enumerate(streams):
        factor = factor_of(sums_ref[a, 0])
        for i in range(LANE_BLOCKS):
            rows = slice(128 * i, 128 * i + 128)
            x = x_ref[rows, :].astype(F32)
            wide_ref[rows, :128] = (x * column(factor[i : i + 1, :]) * gain_ref[0]).astype(BF16)
            if a == 0:
                extra = jnp.where(lane == i, 1.0, 0.0)
            else:
                extra = jnp.broadcast_to(bias_ref[0, i : i + 1, :], (128, 128))
            wide_ref[rows, 128:] = extra.astype(BF16)

    rows = 256

    def scores(c):
        return products(wide_q_ref[rows * c : rows * c + rows, :], wide_k_ref[...])

    def store(c, o):
        out_ref[rows * c : rows * c + rows, :] = o

    attend(LOCATIONS // rows, scores, lambda c: v_ref[...], store)


def frame_attention(query_proj, key_proj, value_proj, sums, gains, bias, head_class):
    tokens = query_proj.shape[0]
    frames = tokens // LOCATIONS
    column_spec = pl.BlockSpec((LOCATIONS, 128), lambda f, c: (f, spatial_head(c)))
    return pl.pallas_call(
        frame_kernel,
        grid_spec=pltpu.PrefetchScalarGridSpec(
            num_scalar_prefetch=1,
            grid=(frames,),
            in_specs=[
                pl.BlockSpec((1, LANE_BLOCKS, 128), lambda f, c: (spatial_head(c), 0, 0)),
                pl.BlockSpec((2, 1, LANE_BLOCKS, 128), lambda f, c: (0, f, 0, 0)),
                pl.BlockSpec((1, 1, 128), lambda f, c: (0, 0, spatial_head(c))),
                pl.BlockSpec((1, 1, 128), lambda f, c: (1, 0, spatial_head(c))),
                column_spec,
                column_spec,
                column_spec,
            ],
            out_specs=pl.BlockSpec((LOCATIONS, 128), lambda f, c: (f, 0)),
            scratch_shapes=[
                pltpu.VMEM((LOCATIONS, 256), BF16),
                pltpu.VMEM((LOCATIONS, 256), BF16),
            ],
        ),
        out_shape=jax.ShapeDtypeStruct((tokens, 128), BF16),
        compiler_params=params(),
        cost_estimate=cost(
            4 * tokens * LOCATIONS * 256, 8 * tokens * 128, tokens * LOCATIONS
        ),
        name="frame_attention",
    )(head_class, bias, sums, gains, gains, query_proj, key_proj, value_proj)


def place_rows(order_ref, moved_ref, heads_ref, rows):
    count, frames = moved_ref.shape[1:3]

    @pl.when(pl.program_id(0) == 0)
    def _():
        for f in range(frames):
            for j in range(count):
                at = 128 * (f * count + j)
                heads_ref[:, at : at + 128] = moved_ref[:, j, f].reshape(LOCATIONS, 128)

    places = lax.broadcasted_iota(jnp.int32, (rows, 128), 0) + pl.program_id(0) * rows
    parts = []
    for i in range(LANE_BLOCKS):
        hit = order_ref[i : i + 1, :] == places
        parts.append(jnp.where(hit, 1.0, 0.0).astype(BF16))
    return jnp.dot(
        jnp.concatenate(parts, axis=1), heads_ref[...], preferred_element_type=F32
    ).astype(BF16)


def join_kernel(class_ref, order_ref, moved_ref, spatial_ref, out_ref, heads_ref):
    frames, rows = out_ref.shape[:2]
    y = place_rows(order_ref, moved_ref, heads_ref, rows)
    for f in range(frames):
        for j in range(TEMPORAL):
            h = pl.multiple_of(temporal_head(class_ref, j) * 128, 128)
            at = 128 * (f * TEMPORAL + j)
            out_ref[f, :, pl.ds(h, 128)] = y[:, at : at + 128]
        h = pl.multiple_of(spatial_head(class_ref) * 128, 128)
        out_ref[f, :, pl.ds(h, 128)] = spatial_ref[f]


def join(returned, spatial_out, head_class, order):
    count, frames = returned.shape[1:3]
    rows = 384
    width = GROUP * 128
    joined = pl.pallas_call(
        join_kernel,
        grid_spec=pltpu.PrefetchScalarGridSpec(
            num_scalar_prefetch=1,
            grid=(LOCATIONS // rows,),
            in_specs=[
                pl.BlockSpec((LANE_BLOCKS, 128), lambda i, c: (0, 0)),
                pl.BlockSpec((16, count, frames, 96, 128), lambda i, c: (0, 0, 0, 0, 0)),
                pl.BlockSpec((frames, rows, 128), lambda i, c: (0, i, 0)),
            ],
            out_specs=pl.BlockSpec((frames, rows, width), lambda i, c: (0, i, 0)),
            scratch_shapes=[pltpu.VMEM((LOCATIONS, frames * count * 128), BF16)],
        ),
        out_shape=jax.ShapeDtypeStruct((frames, LOCATIONS, width), BF16),
        compiler_params=params(),
        cost_estimate=cost(
            2 * frames * LOCATIONS * LOCATIONS * 128 * count, 4 * frames * LOCATIONS * width
        ),
        name="join",
    )(head_class, order, returned, spatial_out.reshape(frames, LOCATIONS, 128))
    return joined.reshape(frames * LOCATIONS, width)


def key_bias(mask):
    blocks = mask.shape[-1]
    same = jnp.arange(blocks)[:, None] == jnp.arange(blocks)[None, :]
    bias = jnp.where((mask != 0) | same, 0.0, MASKED).astype(F32)
    return jnp.pad(jnp.swapaxes(bias, 1, 2), ((0, 0), (0, 0), (0, 128 - blocks)))


def exchange(tensor):
    return lax.all_to_all(tensor, "seq", split_axis=0, concat_axis=0, tiled=True)


def butterfly(sums, step, keep=lambda i: True):
    pairs = [(i, i ^ step) for i in range(lax.axis_size("head")) if keep(i)]
    return sums + lax.ppermute(sums, "head", pairs)


def shards(
    query_proj,
    key_proj,
    value_proj,
    query_gain,
    key_gain,
    head_class,
    spatial_mask,
    temporal_mask,
    location_order,
):
    order = location_order.reshape(LANE_BLOCKS, 128)
    gains = jnp.stack([query_gain, key_gain])[:, None, :]
    window_bias = jnp.repeat(key_bias(temporal_mask), 4, axis=1)
    frame_bias = key_bias(spatial_mask)
    odd = (lax.axis_index("head") % 2).astype(jnp.int32).reshape(1)

    def norms(first, turn, before=None):
        return pack_norms(
            query_proj, key_proj, sums, gains, head_class, order, first, turn, before
        )

    sums = butterfly(square_sums(query_proj, key_proj), 1)
    for step in (2, 4):
        sums = butterfly(sums, step, lambda i: i % 2 == 1)
    first, packed_values = pack_front(
        query_proj, key_proj, value_proj, sums, gains, head_class, order, odd
    )
    packed_values, first, sums = lax.optimization_barrier((packed_values, first, sums))

    values = exchange(packed_values)
    for step in (2, 4):
        sums = butterfly(sums, step, lambda i: i % 2 == 0)
    first = norms(0, 1 - odd, first)
    values, first = lax.optimization_barrier((values, first))

    moved = exchange(first)
    second = norms(PAIR, jnp.ones((1,), jnp.int32))
    spatial_out = frame_attention(
        query_proj, key_proj, value_proj, sums, gains, frame_bias, head_class
    )
    moved, spatial_out, second = lax.optimization_barrier((moved, spatial_out, second))

    moved_later = exchange(second)
    mixed = window_attention(moved, values, window_bias, head_class, 0)
    mixed, moved_later = lax.optimization_barrier((mixed, moved_later))

    mixed = window_attention(moved_later, values, window_bias, head_class, PAIR, mixed)
    return join(exchange(mixed), spatial_out, head_class, order)


def solution(mesh):
    return jax.shard_map(
        shards,
        mesh=mesh,
        in_specs=(
            P("seq", "head"),
            P("seq", "head"),
            P("seq", "head"),
            P("head"),
            P("head"),
            P("head"),
            P("head", None, None),
            P("head", None, None),
            P(),
        ),
        out_specs=P("seq", "head"),
        check_vma=False,
    )
```

```python
import functools

import jax
import jax.numpy as jnp
from jax import lax
from jax.experimental import pallas as pl
from jax.experimental.pallas import tpu as pltpu
from jax.sharding import PartitionSpec as P

HEADS = 40
HEAD_DIM = 128
LOCATIONS = 1536
BLOCK = 128
WINDOW_SPAN = 32
GROUP = 5
TEMPORAL = 4
FEATURES = HEADS * HEAD_DIM
EPSILON = 1e-06
MASKED = -(2.0**100)
EXP2_SCALE = 1.4426950408889634 * HEAD_DIM ** (-0.5)
LANE_BLOCKS = LOCATIONS // 128
PAIR = 2
VMEM_LIMIT = 50 * 2**20

F32 = jnp.float32
BF16 = jnp.bfloat16


def params(vmem=VMEM_LIMIT):
    return pltpu.CompilerParams(vmem_limit_bytes=vmem)


def cost(flops, nbytes, exps=0):
    return pl.CostEstimate(flops=int(flops), bytes_accessed=int(nbytes), transcendentals=int(exps))


def spatial_head(class_ref):
    found = jnp.int32(0)
    for i in range(1, GROUP):
        found = found + i * (1 - class_ref[i])
    return found


def temporal_head(class_ref, j):
    return j + (j >= spatial_head(class_ref)).astype(jnp.int32)


def column(row):
    return jnp.broadcast_to(row, (128, 128)).T


def sums_kernel(q_ref, k_ref, out_ref):
    for a, ref in enumerate((q_ref, k_ref)):
        for i in range(q_ref.shape[0] // 128):
            part = jnp.zeros((128, 128), F32)
            for j in range(GROUP):
                x = ref[128 * i : 128 * i + 128, 128 * j : 128 * j + 128].astype(F32)
                part = part + x * x
            out_ref[a, 0, i, :] = jnp.sum(part.T, axis=0)


def square_sums(query_proj, key_proj):
    tokens, features = query_proj.shape
    frames = tokens // LOCATIONS
    in_spec = pl.BlockSpec((LOCATIONS, features), lambda f: (f, 0))
    return pl.pallas_call(
        sums_kernel,
        grid=(frames,),
        in_specs=[in_spec, in_spec],
        out_specs=pl.BlockSpec((2, 1, LANE_BLOCKS, 128), lambda f: (0, f, 0, 0)),
        out_shape=jax.ShapeDtypeStruct((2, frames, LANE_BLOCKS, 128), F32),
        compiler_params=params(),
        cost_estimate=cost(4 * tokens * features, 4 * tokens * features),
        name="square_sums",
    )(query_proj, key_proj)


def build_picked(order_ref, picked_ref):
    lanes = lax.broadcasted_iota(jnp.int32, (128, 128), 1).astype(F32)

    def body(i, carry):
        wanted = column(order_ref[pl.ds(i, 1), :].astype(F32))
        rows = pl.ds(pl.multiple_of(i * 128, 128), 128)
        for j in range(LANE_BLOCKS):
            hit = wanted == lanes + float(128 * j)
            picked_ref[rows, 128 * j : 128 * j + 128] = jnp.where(hit, 1.0, 0.0).astype(BF16)
        return carry

    lax.fori_loop(0, LANE_BLOCKS, body, 0)


def pick_rows(picked_ref, heads, store):
    rows = 768
    for c in range(LOCATIONS // rows):
        y = jnp.dot(
            picked_ref[rows * c : rows * c + rows, :], heads, preferred_element_type=F32
        ).astype(BF16)
        store(c, rows, y)


def factor_of(sums):
    return lax.rsqrt(sums * (1.0 / FEATURES) + EPSILON)


def norm_steps(first, class_ref, sums_ref, gain_ref, x_refs, out_ref, scratch):
    picked_ref, heads_ref, in_ref, packed_ref, in_sem, out_sem = scratch
    frames = sums_ref.shape[1]
    steps = 2 * frames

    def head(j):
        return pl.multiple_of(temporal_head(class_ref, first + j) * 128, 128)

    def fetch(x_ref, f, n, j):
        return pltpu.make_async_copy(
            x_ref.at[pl.ds(pl.multiple_of(LOCATIONS * f, LOCATIONS), LOCATIONS), pl.ds(head(j), 128)],
            in_ref.at[n * PAIR + j],
            in_sem.at[n * PAIR + j],
        )

    def send(n):
        return pltpu.make_async_copy(
            packed_ref.at[n], out_ref.at[:, :, n // frames, n % frames], out_sem.at[n]
        )

    def arrived(n):
        for j in range(PAIR):
            fetch(x_refs[0], n % frames, n, j).wait()

    def scale(n, i):
        factor = column(factor_of(sums_ref[n // frames, n % frames, i : i + 1, :]))
        rows = slice(128 * i, 128 * i + 128)
        for j in range(PAIR):
            x = in_ref[n * PAIR + j, rows, :].astype(F32)
            gain = gain_ref[n // frames, :, pl.ds(head(j), 128)]
            heads_ref[n % 2, rows, 128 * j : 128 * j + 128] = (x * factor * gain).astype(BF16)

    def products_of(n, also):
        def store(c, rows, y):
            slots = rows // 96
            for j in range(PAIR):
                packed_ref[n, slots * c : slots * c + slots, j] = y[
                    :, 128 * j : 128 * j + 128
                ].reshape(slots, 96, 128)
            if also:
                for i in range(rows * c // 128, rows * (c + 1) // 128):
                    scale(n + 1, i)

        pick_rows(picked_ref, heads_ref[n % 2], store)
        send(n).start()

    def body(n, carry):
        arrived(n + 1)
        products_of(n, True)
        return carry

    for n in range(steps):
        for j in range(PAIR):
            fetch(x_refs[n // frames], n % frames, n, j).start()
    arrived(0)
    for i in range(LANE_BLOCKS):
        scale(0, i)
    lax.fori_loop(0, steps - 1, body, 0)
    products_of(steps - 1, False)
    for n in range(steps):
        send(n).wait()


def pack_norm_kernel(
    first, class_ref, turn_ref, order_ref, sums_ref, gain_ref, q_ref, k_ref, *rest
):
    @pl.when(turn_ref[0] != 0)
    def _():
        build_picked(order_ref, rest[-6])
        norm_steps(first, class_ref, sums_ref, gain_ref, (q_ref, k_ref), rest[-7], rest[-6:])


def front_kernel(
    class_ref, odd_ref, order_ref, sums_ref, gain_ref, q_ref, k_ref, v_ref, *rest
):
    norm_ref, out_ref = rest[:2]
    scratch, (v_in_ref, v_packed_ref, v_in_sem, v_out_sem) = rest[2:8], rest[8:]
    picked_ref = scratch[0]
    frames = sums_ref.shape[1]
    rows = 768
    chunks = LOCATIONS // rows
    slots = rows // 96

    def fetch(f, j):
        h = pl.multiple_of(temporal_head(class_ref, j) * 128, 128)
        return pltpu.make_async_copy(
            v_ref.at[pl.ds(LOCATIONS * f, LOCATIONS), pl.ds(h, 128)],
            v_in_ref.at[f, :, pl.ds(128 * j, 128)],
            v_in_sem.at[f * TEMPORAL + j],
        )

    def send(f, c):
        return pltpu.make_async_copy(
            v_packed_ref.at[f, pl.ds(slots * c, slots)],
            out_ref.at[pl.ds(slots * c, slots), :, f],
            v_out_sem.at[f * chunks + c],
        )

    for f in range(frames):
        for j in range(TEMPORAL):
            fetch(f, j).start()

    build_picked(order_ref, picked_ref)

    @pl.when(odd_ref[0] != 0)
    def _():
        norm_steps(0, class_ref, sums_ref, gain_ref, (q_ref, k_ref), norm_ref, scratch)

    for f in range(frames):
        for j in range(TEMPORAL):
            fetch(f, j).wait()

        def store(c, rows, y):
            for j in range(TEMPORAL):
                v_packed_ref[f, slots * c : slots * c + slots, j] = y[
                    :, 128 * j : 128 * j + 128
                ].reshape(slots, 96, 128)
            send(f, c).start()

        pick_rows(picked_ref, v_in_ref[f], store)
    for f in range(frames):
        for c in range(chunks):
            send(f, c).wait()


def pack_specs(frames, features):
    anywhere = pl.BlockSpec(memory_space=pl.ANY)
    in_specs = [
        pl.BlockSpec((LANE_BLOCKS, 128), lambda i, c, t: (0, 0)),
        pl.BlockSpec((2, frames, LANE_BLOCKS, 128), lambda i, c, t: (0, 0, 0, 0)),
        pl.BlockSpec((2, 1, features), lambda i, c, t: (0, 0, 0)),
        anywhere,
        anywhere,
    ]
    scratch = [
        pltpu.VMEM((LOCATIONS, LOCATIONS), BF16),
        pltpu.VMEM((2, LOCATIONS, PAIR * 128), BF16),
        pltpu.VMEM((2 * frames * PAIR, LOCATIONS, 128), BF16),
        pltpu.VMEM((2 * frames, 16, PAIR, 96, 128), BF16),
        pltpu.SemaphoreType.DMA((2 * frames * PAIR,)),
        pltpu.SemaphoreType.DMA((2 * frames,)),
    ]
    norms = jax.ShapeDtypeStruct((16, PAIR, 2, frames, 96, 128), BF16)
    return in_specs, scratch, norms, anywhere


def pack_front(query_proj, key_proj, value_proj, sums, gains, head_class, order, odd):
    tokens, features = query_proj.shape
    frames = tokens // LOCATIONS
    in_specs, scratch, norms, anywhere = pack_specs(frames, features)
    chunks = LOCATIONS // 768
    return pl.pallas_call(
        front_kernel,
        grid_spec=pltpu.PrefetchScalarGridSpec(
            num_scalar_prefetch=2,
            grid=(1,),
            in_specs=[*in_specs, anywhere],
            out_specs=[anywhere, anywhere],
            scratch_shapes=[
                *scratch,
                pltpu.VMEM((frames, LOCATIONS, TEMPORAL * 128), BF16),
                pltpu.VMEM((frames, 16, TEMPORAL, 96, 128), BF16),
                pltpu.SemaphoreType.DMA((frames * TEMPORAL,)),
                pltpu.SemaphoreType.DMA((frames * chunks,)),
            ],
        ),
        out_shape=[norms, jax.ShapeDtypeStruct((16, TEMPORAL, frames, 96, 128), BF16)],
        compiler_params=params(),
        cost_estimate=cost(6 * tokens * LOCATIONS * 256, 12 * tokens * 256),
        name="pack_front",
    )(head_class, odd, order, sums, gains, query_proj, key_proj, value_proj)


def pack_norms(query_proj, key_proj, sums, gains, head_class, order, first, turn, before=None):
    tokens, features = query_proj.shape
    frames = tokens // LOCATIONS
    in_specs, scratch, norms, anywhere = pack_specs(frames, features)
    operands = [head_class, turn, order, sums, gains, query_proj, key_proj]
    aliases = {}
    if before is not None:
        in_specs.append(anywhere)
        aliases = {len(operands): 0}
        operands.append(before)
    return pl.pallas_call(
        functools.partial(pack_norm_kernel, first),
        grid_spec=pltpu.PrefetchScalarGridSpec(
            num_scalar_prefetch=2,
            grid=(1,),
            in_specs=in_specs,
            out_specs=anywhere,
            scratch_shapes=scratch,
        ),
        out_shape=norms,
        input_output_aliases=aliases,
        compiler_params=params(),
        cost_estimate=cost(4 * tokens * LOCATIONS * 256, 8 * tokens * 256),
        name="pack_norms",
    )(*operands)


def attend(count, scores, values, store):
    s = scores(0)
    for c in range(count):
        later = scores(c + 1) if c + 1 < count else None
        top = jnp.max(s, axis=1, keepdims=True)
        w = jnp.exp2((s - top) * EXP2_SCALE)
        total = jnp.sum(w, axis=1, keepdims=True)
        mixture = jnp.dot(w.astype(BF16), values(c), preferred_element_type=F32)
        store(c, (mixture / total).astype(BF16))
        s = later


def products(queries, key_rows):
    return lax.dot_general(
        queries, key_rows, (((1,), (1,)), ((), ())), preferred_element_type=F32
    )


def window_kernel(class_ref, bias_ref, q_ref, k_ref, v_ref, *rest):
    out_ref, wide_q_ref, wide_k_ref = rest[-3:]
    tokens = 16 * 2 * WINDOW_SPAN
    windows = 96 // WINDOW_SPAN

    @pl.when(pl.program_id(0) == 0)
    def _():
        place = lax.broadcasted_iota(jnp.int32, (tokens, 128), 0) % WINDOW_SPAN
        lane = lax.broadcasted_iota(jnp.int32, (tokens, 128), 1)
        own = jnp.where(place // 4 == lane, 1.0, 0.0).astype(BF16)
        for w in range(windows):
            wide_q_ref[w, :, 128:] = own

    repeated = jnp.broadcast_to(bias_ref[...], (32, WINDOW_SPAN, 128))
    repeated = repeated.reshape(tokens, 128).astype(BF16)
    for w in range(windows):
        rows = slice(WINDOW_SPAN * w, WINDOW_SPAN * w + WINDOW_SPAN)
        wide_q_ref[w, :, :128] = q_ref[:, 0, 0, :, rows, :].reshape(tokens, 128)
        wide_k_ref[w, :, :128] = k_ref[:, 0, 0, :, rows, :].reshape(tokens, 128)
        wide_k_ref[w, :, 128:] = repeated

    rows = 256
    parts = tokens // rows

    def scores(c):
        w, r = divmod(c, parts)
        return products(wide_q_ref[w, rows * r : rows * r + rows, :], wide_k_ref[w])

    def values(c):
        w = c // parts
        return v_ref[:, 0, :, WINDOW_SPAN * w : WINDOW_SPAN * w + WINDOW_SPAN, :].reshape(
            tokens, 128
        )

    def store(c, o):
        w, r = divmod(c, parts)
        slots = rows // (2 * WINDOW_SPAN)
        out_ref[
            slots * r : slots * r + slots, 0, :, WINDOW_SPAN * w : WINDOW_SPAN * w + WINDOW_SPAN, :
        ] = o.reshape(slots, 2, WINDOW_SPAN, 128)

    attend(windows * parts, scores, values, store)


def window_attention(moved, values, bias, head_class, first, before=None):
    count = moved.shape[1]
    windows = 96 // WINDOW_SPAN
    tokens = 16 * 2 * WINDOW_SPAN
    qk_block = (16, 1, 1, 2, 96, 128)
    in_specs = [
        pl.BlockSpec((1, WINDOW_SPAN, 128), lambda h, c: (temporal_head(c, h + first), 0, 0)),
        pl.BlockSpec(qk_block, lambda h, c: (0, h, 0, 0, 0, 0)),
        pl.BlockSpec(qk_block, lambda h, c: (0, h, 1, 0, 0, 0)),
        pl.BlockSpec((16, 1, 2, 96, 128), lambda h, c: (0, h + first, 0, 0, 0)),
    ]
    operands = [head_class, bias, moved, moved, values]
    aliases = {}
    if before is not None:
        in_specs.append(pl.BlockSpec(memory_space=pl.ANY))
        aliases = {len(operands): 0}
        operands.append(before)
    return pl.pallas_call(
        window_kernel,
        grid_spec=pltpu.PrefetchScalarGridSpec(
            num_scalar_prefetch=1,
            grid=(count,),
            in_specs=in_specs,
            out_specs=pl.BlockSpec((16, 1, 2, 96, 128), lambda h, c: (0, h + first, 0, 0, 0)),
            scratch_shapes=[
                pltpu.VMEM((windows, tokens, 256), BF16),
                pltpu.VMEM((windows, tokens, 256), BF16),
            ],
        ),
        out_shape=jax.ShapeDtypeStruct((16, TEMPORAL, 2, 96, 128), BF16),
        input_output_aliases=aliases,
        compiler_params=params(),
        cost_estimate=cost(
            8 * count * windows * tokens * tokens * 128,
            8 * count * windows * tokens * 128,
            count * windows * tokens * tokens,
        ),
        name="window_attention",
    )(*operands)


def frame_kernel(
    class_ref, bias_ref, sums_ref, qg_ref, kg_ref, q_ref, k_ref, v_ref, out_ref, wide_q_ref, wide_k_ref
):
    lane = lax.broadcasted_iota(jnp.int32, (128, 128), 1)
    streams = ((q_ref, qg_ref, wide_q_ref), (k_ref, kg_ref, wide_k_ref))
    for a, (x_ref, gain_ref, wide_ref) in enumerate(streams):
        factor = factor_of(sums_ref[a, 0])
        for i in range(LANE_BLOCKS):
            rows = slice(128 * i, 128 * i + 128)
            x = x_ref[rows, :].astype(F32)
            wide_ref[rows, :128] = (x * column(factor[i : i + 1, :]) * gain_ref[0]).astype(BF16)
            if a == 0:
                extra = jnp.where(lane == i, 1.0, 0.0)
            else:
                extra = jnp.broadcast_to(bias_ref[0, i : i + 1, :], (128, 128))
            wide_ref[rows, 128:] = extra.astype(BF16)

    rows = 256

    def scores(c):
        return products(wide_q_ref[rows * c : rows * c + rows, :], wide_k_ref[...])

    def store(c, o):
        out_ref[rows * c : rows * c + rows, :] = o

    attend(LOCATIONS // rows, scores, lambda c: v_ref[...], store)


def frame_attention(query_proj, key_proj, value_proj, sums, gains, bias, head_class):
    tokens = query_proj.shape[0]
    frames = tokens // LOCATIONS
    column_spec = pl.BlockSpec((LOCATIONS, 128), lambda f, c: (f, spatial_head(c)))
    return pl.pallas_call(
        frame_kernel,
        grid_spec=pltpu.PrefetchScalarGridSpec(
            num_scalar_prefetch=1,
            grid=(frames,),
            in_specs=[
                pl.BlockSpec((1, LANE_BLOCKS, 128), lambda f, c: (spatial_head(c), 0, 0)),
                pl.BlockSpec((2, 1, LANE_BLOCKS, 128), lambda f, c: (0, f, 0, 0)),
                pl.BlockSpec((1, 1, 128), lambda f, c: (0, 0, spatial_head(c))),
                pl.BlockSpec((1, 1, 128), lambda f, c: (1, 0, spatial_head(c))),
                column_spec,
                column_spec,
                column_spec,
            ],
            out_specs=pl.BlockSpec((LOCATIONS, 128), lambda f, c: (f, 0)),
            scratch_shapes=[
                pltpu.VMEM((LOCATIONS, 256), BF16),
                pltpu.VMEM((LOCATIONS, 256), BF16),
            ],
        ),
        out_shape=jax.ShapeDtypeStruct((tokens, 128), BF16),
        compiler_params=params(),
        cost_estimate=cost(
            4 * tokens * LOCATIONS * 256, 8 * tokens * 128, tokens * LOCATIONS
        ),
        name="frame_attention",
    )(head_class, bias, sums, gains, gains, query_proj, key_proj, value_proj)


def place_rows(order_ref, moved_ref, heads_ref, rows):
    count, frames = moved_ref.shape[1:3]

    @pl.when(pl.program_id(0) == 0)
    def _():
        for f in range(frames):
            for j in range(count):
                at = 128 * (f * count + j)
                heads_ref[:, at : at + 128] = moved_ref[:, j, f].reshape(LOCATIONS, 128)

    places = lax.broadcasted_iota(jnp.int32, (rows, 128), 0) + pl.program_id(0) * rows
    parts = []
    for i in range(LANE_BLOCKS):
        hit = order_ref[i : i + 1, :] == places
        parts.append(jnp.where(hit, 1.0, 0.0).astype(BF16))
    return jnp.dot(
        jnp.concatenate(parts, axis=1), heads_ref[...], preferred_element_type=F32
    ).astype(BF16)


def join_kernel(class_ref, order_ref, moved_ref, spatial_ref, out_ref, heads_ref):
    frames, rows = out_ref.shape[:2]
    y = place_rows(order_ref, moved_ref, heads_ref, rows)
    for f in range(frames):
        for j in range(TEMPORAL):
            h = pl.multiple_of(temporal_head(class_ref, j) * 128, 128)
            at = 128 * (f * TEMPORAL + j)
            out_ref[f, :, pl.ds(h, 128)] = y[:, at : at + 128]
        h = pl.multiple_of(spatial_head(class_ref) * 128, 128)
        out_ref[f, :, pl.ds(h, 128)] = spatial_ref[f]


def join(returned, spatial_out, head_class, order):
    count, frames = returned.shape[1:3]
    rows = 768
    width = GROUP * 128
    joined = pl.pallas_call(
        join_kernel,
        grid_spec=pltpu.PrefetchScalarGridSpec(
            num_scalar_prefetch=1,
            grid=(LOCATIONS // rows,),
            in_specs=[
                pl.BlockSpec((LANE_BLOCKS, 128), lambda i, c: (0, 0)),
                pl.BlockSpec((16, count, frames, 96, 128), lambda i, c: (0, 0, 0, 0, 0)),
                pl.BlockSpec((frames, rows, 128), lambda i, c: (0, i, 0)),
            ],
            out_specs=pl.BlockSpec((frames, rows, width), lambda i, c: (0, i, 0)),
            scratch_shapes=[pltpu.VMEM((LOCATIONS, frames * count * 128), BF16)],
        ),
        out_shape=jax.ShapeDtypeStruct((frames, LOCATIONS, width), BF16),
        compiler_params=params(),
        cost_estimate=cost(
            2 * frames * LOCATIONS * LOCATIONS * 128 * count, 4 * frames * LOCATIONS * width
        ),
        name="join",
    )(head_class, order, returned, spatial_out.reshape(frames, LOCATIONS, 128))
    return joined.reshape(frames * LOCATIONS, width)


def key_bias(mask):
    blocks = mask.shape[-1]
    same = jnp.arange(blocks)[:, None] == jnp.arange(blocks)[None, :]
    bias = jnp.where((mask != 0) | same, 0.0, MASKED).astype(F32)
    return jnp.pad(jnp.swapaxes(bias, 1, 2), ((0, 0), (0, 0), (0, 128 - blocks)))


def exchange(tensor):
    return lax.all_to_all(tensor, "seq", split_axis=0, concat_axis=0, tiled=True)


def butterfly(sums, step, keep=lambda i: True):
    pairs = [(i, i ^ step) for i in range(lax.axis_size("head")) if keep(i)]
    return sums + lax.ppermute(sums, "head", pairs)


def shards(
    query_proj,
    key_proj,
    value_proj,
    query_gain,
    key_gain,
    head_class,
    spatial_mask,
    temporal_mask,
    location_order,
):
    order = location_order.reshape(LANE_BLOCKS, 128)
    gains = jnp.stack([query_gain, key_gain])[:, None, :]
    window_bias = jnp.repeat(key_bias(temporal_mask), 4, axis=1)
    frame_bias = key_bias(spatial_mask)
    odd = (lax.axis_index("head") % 2).astype(jnp.int32).reshape(1)

    def norms(first, turn, before=None):
        return pack_norms(
            query_proj, key_proj, sums, gains, head_class, order, first, turn, before
        )

    sums = butterfly(square_sums(query_proj, key_proj), 1)
    for step in (2, 4):
        sums = butterfly(sums, step, lambda i: i % 2 == 1)
    first, packed_values = pack_front(
        query_proj, key_proj, value_proj, sums, gains, head_class, order, odd
    )
    packed_values, first, sums = lax.optimization_barrier((packed_values, first, sums))

    values = exchange(packed_values)
    for step in (2, 4):
        sums = butterfly(sums, step, lambda i: i % 2 == 0)
    first = norms(0, 1 - odd, first)
    values, first = lax.optimization_barrier((values, first))

    moved = exchange(first)
    second = norms(PAIR, jnp.ones((1,), jnp.int32))
    spatial_out = frame_attention(
        query_proj, key_proj, value_proj, sums, gains, frame_bias, head_class
    )
    moved, spatial_out, second = lax.optimization_barrier((moved, spatial_out, second))

    moved_later = exchange(second)
    mixed = window_attention(moved, values, window_bias, head_class, 0)
    mixed, moved_later = lax.optimization_barrier((mixed, moved_later))

    mixed = window_attention(moved_later, values, window_bias, head_class, PAIR, mixed)
    return join(exchange(mixed), spatial_out, head_class, order)


def solution(mesh):
    return jax.shard_map(
        shards,
        mesh=mesh,
        in_specs=(
            P("seq", "head"),
            P("seq", "head"),
            P("seq", "head"),
            P("head"),
            P("head"),
            P("head"),
            P("head", None, None),
            P("head", None, None),
            P(),
        ),
        out_specs=P("seq", "head"),
        check_vma=False,
    )
```
